32 devices in a mesh: req: 8 (over z, y), head: 4 (over x, core).
Axes of the slice: x: 2, y: 2, z: 4, core: 2. Of those that a mesh axis runs over, the one named last changes fastest.
Arguments:
- hidden_in: bfloat16 [128, 2048], P('req'), may hold values from -6 to 6
- lengths: int32 [128], P('req'), may hold values from 1 to 4096, as said below
- page_request: int32 [512], P('req'), may hold values from 0 to 127, as said below
- page_fill: int32 [512], P('req'), may hold values from 0 to 128, as said below
- cache_keys: bfloat16 [512, 4, 128, 128], P('req', 'head'), may hold values from -400 to 400
- cache_values: bfloat16 [512, 4, 128, 128], P('req', 'head'), may hold values from -6 to 6
- attn_gain: float32 [2048], replicated, may hold values from 0.1 to 1.9
- query_weight: bfloat16 [2048, 2048], P(None, 'head'), may hold values from -0.125 to 0.125
- keyval_weight: bfloat16 [2048, 2, 512], P(None, None, 'head'), may hold values from -0.125 to 0.125
- out_weight: bfloat16 [2048, 2048], P('head'), may hold values from -0.125 to 0.125
- moe_gain: float32 [2048], replicated, may hold values from 0.1 to 1.9
- shared_gate_up: bfloat16 [2048, 2, 2816], P(None, None, 'head'), may hold values from -0.125 to 0.125
- shared_down: bfloat16 [2816, 2048], P('head'), may hold values from -0.109375 to 0.109375
- expert_gate_up: bfloat16 [16, 2048, 2, 1408], P('req', None, None, 'head'), may hold values from -0.125 to 0.125
- expert_down: bfloat16 [16, 1408, 2048], P('req', 'head'), may hold values from -0.15625 to 0.15625
- expert_ids: int32 [128, 6], P('req'), may hold values from 0 to 15, all different within a row; in each aligned block of 16 rows (0 to 15, 16 to 31, ...) at most 12 rows name the same one
- route_weights: float32 [128, 6], P('req'), may hold values from 0.1 to 0.6
Outputs:
- layer_out: bfloat16 [128, 2048], P('req', 'head')
The draws below stay inside these ranges and needn't reach their ends.
Inputs may be any that keep to these rules, and one draw needn't show every extreme that they name: `lengths`: some request has exactly 4096 cached tokens. `page_request`: every request owns ceil(lengths / 128) pages, placed anywhere in the pool; the other pages are free. `page_fill`: live tokens fill a page's first slots: 128 in every page of a request but its last, the rest in the last, 0 in a free page. `expert_ids`: among the requests of one index of req no expert is named more than 12 times.
All inputs are finite; a program needn't handle non-finite values.
Results may differ from the reference program's by a relative error of at most 0.023.
Values may be sent and summed in bfloat16 or wider, within the bound.
No kernel may reach another device: no remote copies, remote signals or barrier semaphores. Data moves between devices by JAX's collectives and lax.ppermute only.
A program may use at most 128 MiB of HBM per device.

```python
import math
import jax
import jax.numpy as jnp
import numpy as np
from jax import lax

D = 2048
KVH = 4
QPK = 4
QHEADS = 16
HD = 128
FF = 1408
SHARED_FF = 2816
TOP = 6
EXPERTS = 16
REQ_DEV = 16
REQS = 128
PAGE = 128
MAX_PAGES = 32
PAGES_DEV = 64
PAGES = 512
CAP = 12
N_REQ = 8


def page_layout(key):
    subkeys = jax.random.split(jax.random.fold_in(key, 11), 6)
    top_level = MAX_PAGES.bit_length() - 1
    levels = jnp.minimum(jax.random.randint(subkeys[0], (REQS,), 0, top_level + 1), jax.random.randint(subkeys[1], (REQS,), 0, top_level + 1)).astype(jnp.int32)
    ceiling = jnp.left_shift(jnp.full((REQS,), PAGE, jnp.int32), levels)
    raw_values = jax.random.randint(subkeys[2], (REQS,), 0, 2 ** 30).astype(jnp.int32)
    request_lengths = 1 + raw_values % ceiling
    chosen = jax.random.randint(subkeys[3], (), 0, REQS).astype(jnp.int32)
    indices = jnp.arange(REQS, dtype=jnp.int32)
    request_lengths = jnp.where(indices == chosen, PAGE * MAX_PAGES, request_lengths).astype(jnp.int32)
    counts = (request_lengths + PAGE - 1) // PAGE
    rotation = (indices + chosen) % REQS
    extra_pages = counts[rotation] - 1
    before = jnp.cumsum(extra_pages) - extra_pages
    allowed = jnp.clip(PAGES - REQS - before, 0, extra_pages)
    counts = jnp.zeros((REQS,), jnp.int32).at[rotation].set((1 + allowed).astype(jnp.int32))
    request_lengths = jnp.minimum(request_lengths, counts * PAGE).astype(jnp.int32)
    page_ends = jnp.cumsum(counts).astype(jnp.int32)
    starts = page_ends - counts
    pool_slots = jnp.arange(PAGES, dtype=jnp.int32)
    owners = jnp.sum((page_ends[None, :] <= pool_slots[:, None]).astype(jnp.int32), axis=1).astype(jnp.int32)
    in_use = owners < REQS
    owner_safe = jnp.minimum(owners, REQS - 1)
    within = pool_slots - starts[owner_safe]
    fills = jnp.where(in_use, jnp.clip(request_lengths[owner_safe] - within * PAGE, 0, PAGE), 0).astype(jnp.int32)
    spares = jax.random.randint(subkeys[4], (PAGES,), 0, REQS).astype(jnp.int32)
    requests = jnp.where(in_use, owner_safe, spares).astype(jnp.int32)
    shuffle = jax.random.permutation(subkeys[5], PAGES)
    page_request = jnp.zeros((PAGES,), jnp.int32).at[shuffle].set(requests)
    page_fill = jnp.zeros((PAGES,), jnp.int32).at[shuffle].set(fills)
    return (request_lengths, page_request, page_fill)


def draw_lengths(key, part):
    return page_layout(key)[0]


def draw_page_request(key, part):
    return page_layout(key)[1]


def draw_page_fill(key, part):
    return page_layout(key)[2]


def draw_cache_keys(key, part):
    subkeys = jax.random.split(jax.random.fold_in(key, 23), 1)
    full_shape = (PAGES, KVH, PAGE, HD)
    values = jnp.clip(jax.random.normal(subkeys[0], full_shape, jnp.float32), -6.0, 6.0)
    return values.astype(jnp.bfloat16)


def block_scale(rng, shape, pieces, least, high):
    loudness = 1.0
    for position, blocks in pieces:
        heights = jax.random.uniform(jax.random.fold_in(jax.random.fold_in(rng, 6), position), (blocks,), jnp.float32, least / len(pieces), high / len(pieces))
        loudness = loudness * jnp.repeat(jnp.exp(heights), shape[position] // blocks).reshape((-1,) + (1,) * (len(shape) - 1 - position))
    return loudness


def deal_out(stream_key, own, number, rows, amount, top, bound, slope):
    ranking = jax.random.permutation(stream_key, amount)
    heavy_load, common = shares(amount, rows * top, bound, slope, True), shares(amount, rows * top, bound, slope, False)
    places = jnp.arange(amount)

    def named(tallies, offset_by):
        used = int((tallies > 0).sum())
        fixed = max(1, used // 4)
        moved = fixed + (places - fixed + offset_by * (used - fixed)) % max(1, amount - fixed)
        return jnp.zeros((amount,), jnp.int32).at[ranking[jnp.where(places < fixed, places, moved)]].set(jnp.asarray(tallies, jnp.int32))

    tallies = jnp.where(number % 4 == 0, named(heavy_load, number // 4), named(common, number - number // 4 - 1))
    mixed = jax.random.permutation(jax.random.fold_in(own, 3), amount)
    source_of, taker = mixed[0:amount // 2 * 2:2], mixed[1:amount // 2 * 2:2]
    room = jnp.minimum(tallies[source_of] - 1, bound - tallies[taker]) // 2
    room = jnp.where((source_of == ranking[0]) | (taker == ranking[0]) | (tallies[taker] == 0), 0, jnp.maximum(room, 0))
    moved = jax.random.randint(jax.random.fold_in(own, 4), (amount // 2,), 0, 1 << 20) % (room + 1)
    tallies = tallies.at[source_of].add(-moved).at[taker].add(moved)
    members = jnp.searchsorted(jnp.cumsum(tallies), jnp.arange(rows * top), side="right").astype(jnp.int32)
    listing = members.reshape(top, rows).T
    listing = listing[jax.random.permutation(jax.random.fold_in(own, 1), rows)]
    offset_by = jax.random.randint(jax.random.fold_in(own, 2), (rows, 1), 0, top)
    return jnp.take_along_axis(listing, (jnp.arange(top)[None, :] + offset_by) % top, axis=1)


def shares(number_of, total, reach, skew, full):
    portions = [(1 << 20) // math.isqrt(grade ** skew) + 1 for grade in range(1, number_of + 1)]
    largest = reach if full else min(reach, max(-(-total // number_of), total * portions[0] // sum(portions)))
    least = 1 if total - largest >= number_of - 1 else 0
    holding, spare = [largest] + [least] * (number_of - 1), total - largest - least * (number_of - 1)
    while spare > 0:
        movable = [i for i in range(1, number_of) if holding[i] < largest] or [i for i in range(1, number_of) if holding[i] < reach]
        mass, left = sum([portions[i] for i in movable]), spare
        for i in movable:
            more = min(reach - holding[i], max(1, left * portions[i] // mass), spare)
            holding[i] = holding[i] + more
            spare = spare - more
    return np.array(holding)


def noise(key, dims, deviation, reach, shards=(), kind=jnp.bfloat16):
    gain = block_scale(key, dims, shards, -0.22, 0.18) if shards else 1.0
    entries = jax.random.normal(key, dims, jnp.float32) * deviation * gain
    return jnp.minimum(jnp.maximum(entries, -reach), reach).astype(kind)


def setup_inputs(seed: int = 0) -> dict:
    streams_of = jax.random.split(jax.random.key(seed), 18)
    hidden_in = noise(streams_of[0], (REQS, D), 1.0, 6.0, ((0, 8),))
    lengths = draw_lengths(jax.random.fold_in(streams_of[17], 71), 0)
    page_request = draw_page_request(jax.random.fold_in(streams_of[17], 71), 0)
    page_fill = draw_page_fill(jax.random.fold_in(streams_of[17], 71), 0)
    cache_keys = draw_cache_keys(jax.random.fold_in(streams_of[17], 71), 0)
    cache_values = noise(streams_of[5], (PAGES, KVH, PAGE, HD), 1.0, 6.0, ((0, 8), (1, 4)))
    attn_gain = jnp.clip(1.0 + 0.18 * jax.random.normal(streams_of[6], (D,), jnp.float32), 0.1, 1.9)
    query_weight = noise(streams_of[7], (D, QHEADS * HD), D ** -0.5, 0.125, ((1, 4),))
    keyval_weight = noise(streams_of[8], (D, 2, KVH * HD), D ** -0.5, 0.125, ((2, 4),))
    out_weight = noise(streams_of[9], (QHEADS * HD, D), (QHEADS * HD) ** -0.5, 0.125, ((0, 4),))
    moe_gain = jnp.clip(1.0 + 0.18 * jax.random.normal(streams_of[10], (D,), jnp.float32), 0.1, 1.9)
    shared_gate_up = noise(streams_of[11], (D, 2, SHARED_FF), D ** -0.5, 0.125, ((2, 4),))
    shared_down = noise(streams_of[12], (SHARED_FF, D), SHARED_FF ** -0.5, 0.109375, ((0, 4),))
    expert_gate_up = noise(streams_of[13], (EXPERTS, D, 2, FF), D ** -0.5, 0.125, ((0, 8), (3, 4)))
    expert_down = noise(streams_of[14], (EXPERTS, FF, D), FF ** -0.5, 0.15625, ((0, 8), (1, 4)))
    expert_ids_keys = jax.random.split(jax.random.fold_in(streams_of[15], 1), REQS // REQ_DEV)
    expert_ids_turns = jax.random.permutation(jax.random.fold_in(streams_of[15], 3), REQS // REQ_DEV)
    expert_ids = jax.vmap(lambda own, number: deal_out(jax.random.fold_in(streams_of[15], 2), own, number, REQ_DEV, EXPERTS, TOP, CAP, 2))(expert_ids_keys, expert_ids_turns).reshape((REQS, TOP))
    route_weights = jnp.clip(jnp.exp(math.log(0.6) - 1.7917595 * jax.random.uniform(streams_of[16], (REQS, TOP), jnp.float32) ** block_scale(streams_of[16], (REQS, TOP), ((0, 8),), -0.2, 0.2)), 0.1, 0.6)
    return dict(hidden_in=hidden_in, lengths=lengths, page_request=page_request, page_fill=page_fill, cache_keys=cache_keys, cache_values=cache_values, attn_gain=attn_gain, query_weight=query_weight, keyval_weight=keyval_weight, out_weight=out_weight, moe_gain=moe_gain, shared_gate_up=shared_gate_up, shared_down=shared_down, expert_gate_up=expert_gate_up, expert_down=expert_down, expert_ids=expert_ids, route_weights=route_weights)


EPSILON = 1e-06
ROPE_BASE = 600000.0
NEG_LARGE = -1e+30

def rms_scale(values, gain_vector):
    return values * lax.rsqrt(lax.optimization_barrier(jnp.mean(values * values, axis=-1, keepdims=True)) + EPSILON) * gain_vector

def rotary(values, positions):
    half_dim = values.shape[-1] // 2
    frequency = ROPE_BASE ** (-2.0 * jnp.arange(half_dim, dtype=jnp.float32) / values.shape[-1])
    angles = positions.astype(jnp.float32)[:, None, None] * frequency[None, None, :]
    cosines = jnp.cos(angles)
    sine_part = jnp.sin(angles)
    first_half = values[..., :half_dim]
    second_half = values[..., half_dim:]
    return jnp.concatenate([first_half * cosines - second_half * sine_part, second_half * cosines + first_half * sine_part], axis=-1)

def reference(hidden_in, lengths, page_request, page_fill, cache_keys, cache_values, attn_gain, query_weight, keyval_weight, out_weight, moe_gain, shared_gate_up, shared_down, expert_gate_up, expert_down, expert_ids, route_weights):
    inputs = hidden_in.astype(jnp.float32)
    normed = rms_scale(inputs, attn_gain).astype(jnp.bfloat16)
    query_all = rotary(jnp.dot(normed, query_weight, preferred_element_type=jnp.float32).reshape(REQS, QHEADS, HD), lengths).astype(jnp.bfloat16)
    keyval = jnp.einsum('rd,dkc->rkc', normed.astype(jnp.float32), keyval_weight.astype(jnp.float32))
    new_key = rotary(keyval[:, 0].reshape(REQS, KVH, HD), lengths).astype(jnp.bfloat16)
    new_value = keyval[:, 1].reshape(REQS, KVH, HD).astype(jnp.bfloat16)
    score_scale = HD ** (-0.5)
    page_query = jnp.take(query_all, page_request, axis=0).reshape(N_REQ, PAGES_DEV, KVH, QPK, HD)

    def page_block(operands):
        block_query, block_keys, block_values, block_fill = operands
        scores = jnp.einsum('pgjh,pgth->pgjt', block_query.astype(jnp.float32), block_keys.astype(jnp.float32)) * score_scale
        live_mask = jnp.arange(PAGE, dtype=jnp.int32)[None, None, None, :] < block_fill[:, None, None, None]
        masked = jnp.where(live_mask, scores, NEG_LARGE)
        block_max = lax.optimization_barrier(jnp.max(masked, axis=-1))
        page_probs = jnp.where(live_mask, jnp.exp(masked - block_max[..., None]), 0.0).astype(jnp.bfloat16)
        block_sum = lax.optimization_barrier(jnp.sum(page_probs.astype(jnp.float32), axis=-1))
        block_out = jnp.einsum('pgjt,pgth->pgjh', page_probs.astype(jnp.float32), block_values.astype(jnp.float32))
        return (block_max, block_sum, block_out)
    page_max, page_sum, page_out = lax.map(page_block, (page_query, cache_keys.reshape(N_REQ, PAGES_DEV, KVH, PAGE, HD), cache_values.reshape(N_REQ, PAGES_DEV, KVH, PAGE, HD), page_fill.reshape(N_REQ, PAGES_DEV)))
    page_max = page_max.reshape(PAGES, QHEADS)
    page_sum = page_sum.reshape(PAGES, QHEADS)
    page_out = page_out.reshape(PAGES, QHEADS, HD)
    owner_hot = page_request[:, None] == jnp.arange(REQS, dtype=jnp.int32)[None, :]
    cache_max = lax.optimization_barrier(jnp.max(jnp.where(owner_hot[:, :, None], page_max[:, None, :], NEG_LARGE), axis=0))
    weight = jnp.exp(page_max - jnp.take(cache_max, page_request, axis=0))
    cache_sum = jax.ops.segment_sum(page_sum * weight, page_request, num_segments=REQS)
    cache_out = jax.ops.segment_sum(page_out * weight[:, :, None], page_request, num_segments=REQS)
    key_rows = jnp.repeat(new_key, QPK, axis=1).astype(jnp.float32)
    value_rows = jnp.repeat(new_value, QPK, axis=1).astype(jnp.float32)
    new_score = lax.optimization_barrier(jnp.sum(query_all.astype(jnp.float32) * key_rows, axis=-1)) * score_scale
    total_max = jnp.maximum(cache_max, new_score)
    old_scale = jnp.exp(cache_max - total_max)
    new_scale = jnp.exp(new_score - total_max)
    denominator = cache_sum * old_scale + new_scale
    numerator = cache_out * old_scale[..., None] + new_scale[..., None] * value_rows
    attention = (numerator / denominator[..., None]).reshape(REQS, QHEADS * HD).astype(jnp.bfloat16)
    residual = inputs + jnp.dot(attention, out_weight, preferred_element_type=jnp.float32)
    moe_input = rms_scale(residual, moe_gain).astype(jnp.bfloat16)
    shared_pair = jnp.einsum('rd,dkf->rkf', moe_input.astype(jnp.float32), shared_gate_up.astype(jnp.float32))
    shared_act = (jax.nn.silu(shared_pair[:, 0]) * shared_pair[:, 1]).astype(jnp.bfloat16)
    shared_out = jnp.dot(shared_act, shared_down, preferred_element_type=jnp.float32)
    flat_ids = expert_ids.reshape(N_REQ, REQ_DEV * TOP)
    expert_hot = (flat_ids[:, :, None] == jnp.arange(EXPERTS, dtype=jnp.int32)[None, None, :]).astype(jnp.int32)
    slot_ranks = lax.optimization_barrier(jnp.sum((jnp.cumsum(expert_hot, axis=1) - expert_hot) * expert_hot, axis=2)).astype(jnp.int32)
    blocks = jnp.arange(N_REQ, dtype=jnp.int32)[:, None]
    slot_ids = ((flat_ids * N_REQ + blocks) * CAP + slot_ranks).reshape(REQS * TOP).astype(jnp.int32)
    token_ids = (jnp.arange(REQS * TOP, dtype=jnp.int32) // TOP).astype(jnp.int32)
    slot_table = jnp.zeros((EXPERTS * N_REQ * CAP,), jnp.int32).at[slot_ids].set(token_ids)
    expert_rows = jnp.take(moe_input, slot_table, axis=0).reshape(EXPERTS, N_REQ * CAP, D)

    def run_expert(operands):
        rows_in, pair_weight, down_weight = operands
        pair = jnp.dot(rows_in, pair_weight.reshape(D, 2 * FF), preferred_element_type=jnp.float32).reshape(N_REQ * CAP, 2, FF)
        expert_act = (jax.nn.silu(pair[:, 0]) * pair[:, 1]).astype(jnp.bfloat16)
        return jnp.dot(expert_act, down_weight, preferred_element_type=jnp.float32)
    expert_out = lax.map(run_expert, (expert_rows, expert_gate_up, expert_down)).reshape(EXPERTS * N_REQ * CAP, D)
    picked = jnp.take(expert_out, slot_ids, axis=0).reshape(REQS, TOP, D)
    routed = lax.optimization_barrier(jnp.sum(route_weights[:, :, None] * picked, axis=1))
    return (residual + shared_out + routed).astype(jnp.bfloat16)
```

```python
import functools
import math

import jax
import jax.numpy as jnp
import numpy as np
from jax import lax
from jax.experimental import pallas as pl
from jax.experimental.pallas import tpu as pltpu
from jax.sharding import Mesh
from jax.sharding import PartitionSpec as P

QPK = 4
HD = 128

EPSILON = 1e-06
ROPE_BASE = 600000.0
NEG_LARGE = -1e30
BF = jnp.bfloat16
F32 = jnp.float32
I32 = jnp.int32
VMEM = pl.BlockSpec(memory_space=pltpu.VMEM)
HBM = pl.BlockSpec(memory_space=pltpu.HBM)
REQ = ("ru", "rl")
HEAD = ("hu", "hl")
NT = (((1,), (1,)), ((), ()))
TN = (((0,), (0,)), ((), ()))


def rms_scale(values, gain_vector):
    return (
        values
        * lax.rsqrt(jnp.mean(values * values, axis=-1, keepdims=True) + EPSILON)
        * gain_vector
    )


def index_of(axes):
    return lax.axis_index(axes[0]) * lax.axis_size(axes[1]) + lax.axis_index(axes[1])


def size_of(axes):
    return lax.axis_size(axes[0]) * lax.axis_size(axes[1])


def swap(value, req_step, head_step=0):
    heads = size_of(HEAD)
    count = size_of(REQ) * heads
    step = req_step * heads + head_step
    return lax.ppermute(value, REQ + HEAD, [(i, i ^ step) for i in range(count)])


def stages(count, first):
    found, shift = [], 0
    while count > 1:
        size = min(count, 4 if shift else first)
        found.append((shift, size))
        shift += size.bit_length() - 1
        count //= size
    return found


def trade(whole, half, shift):
    heads = size_of(HEAD)
    count = size_of(REQ) * heads
    steps = [(2 << shift) * heads, (3 << shift) * heads]
    came = lax.ppermute(whole, REQ + HEAD, [(i, i ^ steps[i % 2]) for i in range(count)])
    return jnp.concatenate([half, came, swap(half, 1 << shift)], axis=0)


def position(index, plan):
    place, scale = 0, 1
    for shift, size in reversed(plan):
        place = place + ((index >> shift) & (size - 1)) * scale
        scale *= size
    return place


def gather(block, plan):
    for shift, size in reversed(plan):
        block = jnp.concatenate(
            [block] + [swap(block, i << shift) for i in range(1, size)], axis=0
        )
    return block


def joined(*arrays):
    return lax.optimization_barrier(arrays)


def deliver(blocks, plan):
    for shift, size in plan:
        part = blocks.shape[1] // size
        blocks = jnp.concatenate(
            [blocks[:, :part]]
            + [swap(blocks[:, i * part : (i + 1) * part], i << shift) for i in range(1, size)],
            axis=0,
        )
    return blocks


def scatter(blocks, plan):
    for shift, size in plan:
        part = blocks.shape[0] // size
        total = blocks[:part]
        for i in (size - 1, *range(1, size - 1)):
            sent = blocks[i * part : (i + 1) * part].astype(BF)
            total = total + swap(sent, i << shift).astype(F32)
        blocks = total
    return blocks


def call(kernel, out_shape, args, specs=None, scratch=(), mib=24, flops=0, nbytes=0):
    return pl.pallas_call(
        kernel,
        out_shape=out_shape,
        in_specs=specs or [VMEM] * len(args),
        out_specs=jax.tree.map(lambda _: VMEM, out_shape),
        scratch_shapes=list(scratch),
        compiler_params=pltpu.CompilerParams(vmem_limit_bytes=mib << 20),
        cost_estimate=pl.CostEstimate(flops=flops, bytes_accessed=nbytes, transcendentals=0),
    )(*args)


def in_hbm(*arrays):
    return tuple(pltpu.with_memory_space_constraint(a, pltpu.HBM) for a in arrays)


def stage(parts, *refs):
    count = len(parts)
    sources = [r if p is None else r.at[p] for r, p in zip(refs[1 : 1 + count], parts)]
    copies = fetch(list(zip(sources, refs[1 + count : -1])), refs[-1])
    for copy in copies:
        copy.wait()


def staged(after, *pairs):
    arrays, parts = zip(*[p if isinstance(p, tuple) else (p, None) for p in pairs])
    shapes = [a.shape if p is None else a.shape[1:] for a, p in zip(arrays, parts)]
    return call(
        functools.partial(stage, parts),
        tuple(pltpu.VMEM(shape, a.dtype) for shape, a in zip(shapes, arrays)),
        (after,) + in_hbm(*arrays),
        specs=[HBM] * (1 + len(arrays)),
        scratch=(pltpu.SemaphoreType.DMA((len(arrays),)),),
        mib=1,
        nbytes=sum(2 * math.prod(shape) for shape in shapes),
    )


def fetch(pairs, sem):
    copies = [pltpu.make_async_copy(a, b, sem.at[i]) for i, (a, b) in enumerate(pairs)]
    for copy in copies:
        copy.start()
    return copies


def cos_sin(angle):
    turns = jnp.floor(angle * (2.0 / 3.141592653589793) + 0.5)
    rest = angle - turns * 1.5703125
    rest = rest - turns * 4.837512969970703125e-4
    rest = rest - turns * 7.54978995489188216e-8
    square = rest * rest
    sine = ((-1.9515295891e-4 * square + 8.3321608736e-3) * square - 1.6666654611e-1) * square
    sine = sine * rest + rest
    cosine = (2.443315711809948e-5 * square - 1.388731625493765e-3) * square + 4.166664568298827e-2
    cosine = cosine * square * square - 0.5 * square + 1.0
    turns = turns.astype(I32)
    odd = (turns & 1) == 1
    cosine, sine = jnp.where(odd, sine, cosine), jnp.where(odd, cosine, sine)
    cosine = jnp.where(((turns + 1) & 2) == 2, -cosine, cosine)
    sine = jnp.where((turns & 2) == 2, -sine, sine)
    return cosine, sine


def project(
    lengths_hbm, freq_hbm, ids_hbm, route_hbm, hidden_hbm, gain_hbm, weight_hbm, out_ref, turn_ref, norm_ref,
    lengths, freq, ids, routes, hidden, gain, weight, sem,
):
    chunks = sem.shape[0] - 6
    deep = weight.shape[0] // chunks
    parts = [pl.ds(i * deep, deep) for i in range(chunks)]
    *heavy, early, late, first, second, third, last = fetch(
        [(weight_hbm.at[p], weight.at[p]) for p in parts]
        + [
            (lengths_hbm, lengths),
            (freq_hbm, freq),
            (ids_hbm, ids),
            (route_hbm, routes),
            (hidden_hbm, hidden),
            (gain_hbm, gain),
        ],
        sem,
    )
    copies = [early, late, first, second, third, last, *heavy]
    width = weight.shape[1]
    rows = hidden.shape[0]
    copies[0].wait()
    copies[1].wait()
    diagonal = lax.broadcasted_iota(I32, (rows, rows), 0) == lax.broadcasted_iota(
        I32, (rows, rows), 1
    )
    positions = jnp.sum(
        jnp.where(diagonal, lengths[...].astype(F32), 0.0), axis=1, keepdims=True
    )
    cosine, sine = cos_sin(positions * freq[...])
    sine = jnp.where(lax.broadcasted_iota(I32, sine.shape, 1) < HD // 2, -sine, sine)
    turn_ref[:, :HD] = cosine
    turn_ref[:, HD : 2 * HD] = sine
    core = lax.axis_index(HEAD[1]).astype(F32)
    turn_ref[:, 2 * HD :] = jnp.broadcast_to(core, (rows, HD))
    copies[2].wait()
    copies[3].wait()
    route = routes[...]
    heavy = route.astype(BF).astype(F32)
    lines = jnp.concatenate([ids[...].astype(F32), heavy, route - heavy], axis=0).astype(BF)
    shape = (lines.shape[0], HD)
    eye = lax.broadcasted_iota(I32, shape, 0) == lax.broadcasted_iota(I32, shape, 1)
    out_ref[:, width:] = lax.dot_general(
        lines, jnp.where(eye, 1.0, 0.0).astype(BF), TN, preferred_element_type=F32
    ).astype(BF)
    copies[4].wait()
    copies[5].wait()
    normed = rms_scale(hidden[...].astype(F32), gain[...]).astype(BF)
    norm_ref[...] = normed
    query = jnp.zeros((rows, width), F32)
    for i in range(chunks):
        copies[6 + i].wait()
        part = slice(i * deep, (i + 1) * deep)
        query = query + jnp.dot(normed[:, part], weight[part], preferred_element_type=F32)
    for i in range(width // HD):
        part = query[:, i * HD : (i + 1) * HD]
        turned = part * cosine + pltpu.roll(part, HD // 2, 1) * sine
        out_ref[:, i * HD : (i + 1) * HD] = turned.astype(BF)


def attend(
    query_ref, column_ref, row_ref, fill_ref, keys, values, out_ref,
    scores, probs, out_buf,
):
    pages = keys.shape[0]
    rows = query_ref.shape[0]
    lines = pages * QPK
    slots = keys.shape[1]
    hot = lax.broadcasted_iota(I32, (lines, QPK * rows), 1) == column_ref[...]
    stacked = jnp.concatenate([query_ref[:, i * HD : (i + 1) * HD] for i in range(QPK)], axis=0)
    query = jnp.dot(
        jnp.where(hot, 1.0, 0.0).astype(BF), stacked, preferred_element_type=F32
    ).astype(BF)
    some = 4
    span = some * slots
    for g in range(pages // some):
        part = slice(g * some * QPK, (g + 1) * some * QPK)
        key = keys[g * some : (g + 1) * some].reshape(span, HD)
        scores[part] = lax.dot_general(query[part], key, NT, preferred_element_type=F32)
    slot = lax.broadcasted_iota(I32, (lines, span), 1)
    first = (lax.broadcasted_iota(I32, (lines, 1), 0) // QPK) % some * slots
    live = (slot >= first) & (slot < first + fill_ref[...])
    score = jnp.where(live, scores[...] * (HD ** (-0.5)), NEG_LARGE)
    page_max = jnp.max(score, axis=1, keepdims=True)
    prob = jnp.where(live, jnp.exp(score - page_max), 0.0).astype(BF)
    probs[...] = prob
    page_sum = jnp.sum(prob.astype(F32), axis=1, keepdims=True)
    for g in range(pages // some):
        part = slice(g * some * QPK, (g + 1) * some * QPK)
        value = values[g * some : (g + 1) * some].reshape(span, HD)
        out_buf[part] = jnp.dot(probs[part], value, preferred_element_type=F32)
    held_max = jnp.max(jnp.where(hot, page_max, NEG_LARGE), axis=0, keepdims=True)
    back = jnp.sum(jnp.where(hot, held_max, 0.0), axis=1, keepdims=True)
    weight = jnp.exp(page_max - back)
    held_sum = jnp.sum(jnp.where(hot, page_sum * weight, 0.0), axis=0, keepdims=True)
    turned = lax.broadcasted_iota(I32, (QPK * rows, lines), 0) == row_ref[...]
    held_out = jnp.dot(
        jnp.where(turned, 1.0, 0.0).astype(BF),
        (out_buf[...] * weight).astype(BF),
        preferred_element_type=F32,
    )
    for i in range(QPK):
        out_ref[:, i * HD : (i + 1) * HD] = held_out[i * rows : (i + 1) * rows].astype(BF)
    rest = jnp.concatenate(
        [held_max[:, i * rows : (i + 1) * rows] for i in range(QPK)]
        + [held_sum[:, i * rows : (i + 1) * rows] for i in range(QPK)],
        axis=0,
    )
    terms = []
    for _ in range(3):
        term = rest.astype(BF).astype(F32)
        terms.append(term)
        rest = rest - term
    terms.append(jnp.zeros((HD - 6 * QPK, rows), F32))
    out_ref[:, QPK * HD :] = jnp.concatenate(terms, axis=0).T.astype(BF)


def combine(
    came_ref, query_ref, kv_ref, weight_ref, keep_ref, send_ref
):
    sources, rows = came_ref.shape[0], came_ref.shape[1]
    stats = came_ref[:, :, QPK * HD :].astype(F32).reshape(sources * rows, HD)
    step = 2 * QPK
    stats = stats[:, :step] + stats[:, step : 2 * step] + stats[:, 2 * step : 3 * step]
    stats = stats.reshape(sources, rows, step)
    part_max, part_sum = stats[:, :, :QPK], stats[:, :, QPK:]
    own_max = jnp.max(part_max, axis=0)
    key = kv_ref[:, :HD].astype(F32)
    value = kv_ref[:, HD:].astype(F32)
    new_score = jnp.concatenate(
        [
            jnp.sum(query_ref[:, i * HD : (i + 1) * HD].astype(F32) * key, axis=1, keepdims=True)
            for i in range(QPK)
        ],
        axis=1,
    ) * (HD ** (-0.5))
    top = jnp.maximum(own_max, new_score)
    new_scale = jnp.exp(new_score - top)
    scale = jnp.exp(part_max - top[None])
    denominator = jnp.sum(scale * part_sum, axis=0) + new_scale
    attention = []
    for i in range(QPK):
        total = new_scale[:, i : i + 1] * value
        for s in range(sources):
            total = total + scale[s, :, i : i + 1] * came_ref[
                s, :, i * HD : (i + 1) * HD
            ].astype(F32)
        attention.append((total / denominator[:, i : i + 1]).astype(BF))
    wide = jnp.dot(
        jnp.concatenate(attention, axis=1), weight_ref[...], preferred_element_type=F32
    )
    keep_ref[...] = wide
    send_ref[...] = wide.astype(BF)


def shared_kernel(
    residual_ref, gain_ref, gate_ref, down_ref, up_hbm, out_ref, up_ref, sem
):
    copies = fetch(((up_hbm.at[1], up_ref),), sem)
    inputs = rms_scale(residual_ref[...], gain_ref[...]).astype(BF)
    gate = lax.dot_general(inputs, gate_ref[...], NT, preferred_element_type=F32)
    copies[0].wait()
    up = lax.dot_general(inputs, up_ref[...], NT, preferred_element_type=F32)
    act = (jax.nn.silu(gate) * up).astype(BF)
    out_ref[...] = jnp.dot(act, down_ref[...], preferred_element_type=F32)


def blocks_of(step):
    head = index_of(HEAD)
    return lambda i, size: pl.ds(pl.multiple_of((head ^ (2 * i + step)) * size, HD), size)


def down_product(acts, down, shared_ref, out_ref, step):
    few = shared_ref.shape[0]
    size = out_ref.shape[2]
    place = blocks_of(step)
    for i in range(out_ref.shape[0]):
        at = place(i, size)
        out = sum(
            jnp.dot(act[...], down[e, :, at], preferred_element_type=F32)
            for e, act in enumerate(acts)
        )
        out_ref[i, :few] = (out[:few] + shared_ref[:, at]).astype(out_ref.dtype)
        out_ref[i, few:] = out[few:].astype(out_ref.dtype)


def keep_kernel(acts_ref, down_ref, shared_ref, keep_ref):
    acts = [acts_ref.at[e] for e in range(acts_ref.shape[0])]
    down_product(acts, down_ref, shared_ref, keep_ref, 0)


def experts_kernel(routes, count, *refs):
    here, there, here_other, there_other, gain_ref, routing_ref, shared_ref = refs[:7]
    expert_up = refs[7 : 7 + count]
    down_hbm, send_ref, acts_ref, down_ref, inputs, squares, sem = refs[7 + count :]
    copies = fetch([(down_hbm.at[e], down_ref.at[e]) for e in range(count)], sem)
    lines, size = here.shape
    core = lax.axis_index(HEAD[1])
    few = shared_ref.shape[0]
    squares[...] = jnp.zeros(squares.shape, F32)

    def put(rows, columns, values):
        values = values.astype(F32)
        squares[rows] += jnp.sum(values * values, axis=1, keepdims=True)
        inputs[rows, columns] = (values * gain_ref[:, columns]).astype(BF)

    for y, pair in enumerate(((here, here_other), (there, there_other))):
        for c, ref in zip((core, 1 - core), pair):
            half = pl.ds(pl.multiple_of(c * size, HD), size)
            for k in range(0, lines, 4 * few):
                row = y * lines + k
                third = pl.ds(pl.multiple_of(row + (2 + c) * few, 16), few)
                put(pl.ds(row, few), half, ref[k : k + few])
                put(third, pl.ds(0, size), ref[k + few : k + 2 * few])
                put(third, pl.ds(size, size), ref[k + 2 * few : k + 3 * few])
                put(pl.ds(row + few, few), half, ref[k + 3 * few : k + 4 * few])
    scale = lax.rsqrt(squares[:, :1] / (2 * size) + EPSILON)
    routing = routing_ref[...].astype(F32)
    ids = routing[:, :routes]
    weights = routing[:, routes : 2 * routes] + routing[:, 2 * routes : 3 * routes]
    for e in range(count):
        index = (index_of(REQ) * count + e).astype(F32)
        factor = jnp.sum(jnp.where(ids == index, weights, 0.0), axis=1, keepdims=True)
        gate = lax.dot_general(inputs[...], expert_up[e][0], NT, preferred_element_type=F32)
        up = lax.dot_general(inputs[...], expert_up[e][1], NT, preferred_element_type=F32)
        act = jax.nn.silu(gate * scale) * (up * scale) * factor
        acts_ref[e] = act.astype(BF)
    for copy in copies:
        copy.wait()
    acts = [acts_ref.at[e] for e in range(count)]
    down_product(acts, down_ref, shared_ref, send_ref, 1)


def local(
    hidden_in,
    lengths,
    page_request,
    page_fill,
    cache_keys,
    cache_values,
    attn_gain,
    query_weight,
    keyval_weight,
    out_weight,
    moe_gain,
    shared_gate_up,
    shared_down,
    expert_gate_up,
    expert_down,
    expert_ids,
    route_weights,
):
    rows, width = hidden_in.shape
    req_count = size_of(REQ)
    head_count = size_of(HEAD)
    req = index_of(REQ)
    wide = QPK * HD
    all_rows = rows * req_count
    pages = page_request.shape[0]
    top = expert_ids.shape[1]
    quarter = width // head_count
    plan = stages(req_count, 2)
    far = head_count // 2

    half = HD // 2
    frequency = np.tile(ROPE_BASE ** (-2.0 * np.arange(half) / HD), 2).astype(np.float32)[None]

    def vmem(*shape, dtype=BF):
        return pltpu.VMEM(shape, dtype)

    inputs = in_hbm(
        lengths[None],
        jnp.asarray(frequency),
        expert_ids.T,
        route_weights.T,
        hidden_in,
        attn_gain[None],
        query_weight,
    )
    packed, turn, normed = call(
        project,
        (
            jax.ShapeDtypeStruct((rows, wide + HD), BF),
            jax.ShapeDtypeStruct((rows, 3 * HD), F32),
            jax.ShapeDtypeStruct((rows, width), BF),
        ),
        inputs,
        specs=[HBM] * 7,
        scratch=tuple(pltpu.VMEM(a.shape, a.dtype) for a in inputs)
        + (pltpu.SemaphoreType.DMA((10,)),),
        flops=2 * rows * width * wide,
        nbytes=2 * width * wide,
    )
    shape = (pages, cache_keys.shape[2], HD)
    near = gather(packed, plan[1:])
    keyval = jnp.einsum("rd,dkc->rkc", normed, keyval_weight, preferred_element_type=F32)
    new_key = keyval[:, 0]
    new_key = new_key * turn[:, :HD] + jnp.roll(new_key, half, axis=1) * turn[:, HD : 2 * HD]
    new_kv = jnp.concatenate([new_key, keyval[:, 1]], axis=1).astype(BF)
    near, new_kv = joined(near, new_kv)
    keys, values = staged(near, cache_keys.reshape(shape), cache_values.reshape(shape))
    gathered = gather(near, plan[:1])

    place = position((page_request // rows) ^ req, plan) * rows + page_request % rows
    block = jnp.arange(QPK, dtype=I32)[None, :] * all_rows
    column = (block + place[:, None]).reshape(-1)
    fill = jnp.repeat(page_fill, QPK)
    partial = call(
        attend,
        jax.ShapeDtypeStruct((all_rows, wide + HD), BF),
        (gathered, column[:, None], column[None, :], fill[:, None], keys, values),
        scratch=(
            vmem(pages * QPK, 4 * shape[1], dtype=F32),
            vmem(pages * QPK, 4 * shape[1]),
            vmem(pages * QPK, HD, dtype=F32),
        ),
        flops=4 * pages * QPK * 4 * shape[1] * HD,
        nbytes=4 * pages * shape[1] * HD,
    )
    shared_up = jnp.transpose(shared_gate_up, (1, 2, 0))
    expert_up = jnp.transpose(expert_gate_up, (0, 2, 3, 1))
    experts = expert_up.shape[0]
    early = experts // 2
    out_w, *ups = staged(partial, out_weight, *[(expert_up, e) for e in range(early)])
    came = deliver(partial[None], plan[:1])
    came, out_w, *ups = joined(came, out_w, *ups)
    ups += staged(came, *[(expert_up, e) for e in range(early, experts)])
    came = deliver(came, plan[1:])
    came, *ups = joined(came, *ups)

    keep, send = call(
        combine,
        (jax.ShapeDtypeStruct((rows, width), F32), jax.ShapeDtypeStruct((rows, width), BF)),
        (came, packed, new_kv, out_w),
        flops=2 * rows * wide * width,
        nbytes=2 * wide * width,
        mib=8,
    )
    keep = keep + swap(send, 0, 1).astype(F32)
    sent = keep.astype(BF)
    (shared_down,) = staged(sent, shared_down)
    residual = keep + hidden_in.astype(F32)
    for i in range(1, far):
        residual = residual + swap(sent, 0, 2 * i).astype(F32)
    residual, shared_down = joined(residual, shared_down)

    (gate_w,) = staged(residual, (shared_up, 0))
    core = turn[:, 2 * HD : 2 * HD + 1]
    half_width = width // 2
    low = residual.astype(BF)
    sides = (low[:, :half_width], low[:, half_width:])
    here = trade(
        jnp.concatenate(sides, axis=0), jnp.where(core > 0.5, sides[1], sides[0]), plan[-1][0]
    )
    here = gather(here, plan[1:-1])
    here, late, gate_w = joined(here, residual, gate_w)
    there = swap(here, 1)
    here_other = swap(here, 0, 1)
    shared = call(
        shared_kernel,
        jax.ShapeDtypeStruct((rows, width), F32),
        (late, moe_gain[None], gate_w, shared_down) + in_hbm(shared_up),
        specs=[VMEM] * 4 + [HBM],
        scratch=(vmem(*shared_down.shape), pltpu.SemaphoreType.DMA((1,))),
        flops=6 * rows * width * shared_down.shape[0],
        nbytes=6 * width * shared_down.shape[0],
        mib=12,
    )
    there, shared = joined(there, shared)
    there_other = swap(there, 0, 1)

    small = (here, there, here_other, there_other, moe_gain[None], gathered[:, wide:], shared)
    blocks = (far, all_rows, quarter)
    send, acts, down = call(
        functools.partial(experts_kernel, top, experts),
        (
            jax.ShapeDtypeStruct(blocks, BF),
            jax.ShapeDtypeStruct((experts, all_rows, expert_down.shape[1]), BF),
            pltpu.VMEM(expert_down.shape, BF),
        ),
        small + tuple(ups) + in_hbm(expert_down),
        specs=[VMEM] * (7 + experts) + [HBM],
        scratch=(
            vmem(all_rows, width),
            vmem(all_rows, HD, dtype=F32),
            pltpu.SemaphoreType.DMA((experts,)),
        ),
        flops=5 * all_rows * width * 2 * expert_down.shape[1],
        nbytes=5 * width * 2 * expert_down.shape[1],
    )
    keep = call(
        keep_kernel,
        jax.ShapeDtypeStruct(blocks, F32),
        (acts, down, shared),
        flops=all_rows * width * 2 * expert_down.shape[1],
        nbytes=width * 2 * expert_down.shape[1],
        mib=16,
    )
    keep = keep + swap(send, 0, 1).astype(F32)
    part = all_rows // 2
    total = keep[0, :part]
    for i in reversed(range(far)):
        for j in (1, 0):
            if i or j:
                sent = keep[i, j * part : (j + 1) * part].astype(BF)
                total = total + swap(sent, j, 2 * i).astype(F32)
    total = scatter(total, plan[1:])
    own = lax.dynamic_slice_in_dim(residual, index_of(HEAD) * quarter, quarter, 1)
    return (own + total).astype(BF)


def solution(mesh):
    in_specs = (
        P("req", None),
        P("req"),
        P("req"),
        P("req"),
        P("req", "head", None, None),
        P("req", "head", None, None),
        P(),
        P(None, "head"),
        P(None, None, "head"),
        P("head", None),
        P(),
        P(None, None, "head"),
        P("head", None),
        P("req", None, None, "head"),
        P("req", "head", None),
        P("req", None),
        P("req", None),
    )
    out_specs = P("req", "head")
    shape = (mesh.shape["req"] // 2, 2, mesh.shape["head"] // 2, 2)
    split = Mesh(mesh.devices.reshape(shape), REQ + HEAD)
    names = {"req": REQ, "head": HEAD}
    in_specs, out_specs = jax.tree.map(
        lambda spec: P(*(names.get(n) for n in spec)),
        (in_specs, out_specs),
        is_leaf=lambda spec: isinstance(spec, P),
    )
    return jax.shard_map(local, mesh=split, in_specs=in_specs, out_specs=out_specs, check_vma=False)
```

```python
import functools
import math

import jax
import jax.numpy as jnp
import numpy as np
from jax import lax
from jax.experimental import pallas as pl
from jax.experimental.pallas import tpu as pltpu
from jax.sharding import Mesh
from jax.sharding import PartitionSpec as P

QPK = 4
HD = 128

EPSILON = 1e-06
ROPE_BASE = 600000.0
NEG_LARGE = -1e30
BF = jnp.bfloat16
F32 = jnp.float32
I32 = jnp.int32
VMEM = pl.BlockSpec(memory_space=pltpu.VMEM)
HBM = pl.BlockSpec(memory_space=pltpu.HBM)
REQ = ("ru", "rl")
HEAD = ("hu", "hl")
NT = (((1,), (1,)), ((), ()))
TN = (((0,), (0,)), ((), ()))


def rms_scale(values, gain_vector):
    return (
        values
        * lax.rsqrt(jnp.mean(values * values, axis=-1, keepdims=True) + EPSILON)
        * gain_vector
    )


def index_of(axes):
    return lax.axis_index(axes[0]) * lax.axis_size(axes[1]) + lax.axis_index(axes[1])


def size_of(axes):
    return lax.axis_size(axes[0]) * lax.axis_size(axes[1])


def swap(value, req_step, head_step=0):
    heads = size_of(HEAD)
    count = size_of(REQ) * heads
    step = req_step * heads + head_step
    return lax.ppermute(value, REQ + HEAD, [(i, i ^ step) for i in range(count)])


def stages(count, first):
    found, shift = [], 0
    while count > 1:
        size = min(count, 4 if shift else first)
        found.append((shift, size))
        shift += size.bit_length() - 1
        count //= size
    return found


def trade(whole, half, shift):
    heads = size_of(HEAD)
    count = size_of(REQ) * heads
    steps = [(2 << shift) * heads, (3 << shift) * heads]
    came = lax.ppermute(whole, REQ + HEAD, [(i, i ^ steps[i % 2]) for i in range(count)])
    return jnp.concatenate([half, came, swap(half, 1 << shift)], axis=0)


def position(index, plan):
    place, scale = 0, 1
    for shift, size in reversed(plan):
        place = place + ((index >> shift) & (size - 1)) * scale
        scale *= size
    return place


def gather(block, plan):
    for shift, size in reversed(plan):
        block = jnp.concatenate(
            [block] + [swap(block, i << shift) for i in range(1, size)], axis=0
        )
    return block


def joined(*arrays):
    return lax.optimization_barrier(arrays)


def deliver(blocks, plan):
    for shift, size in plan:
        part = blocks.shape[1] // size
        blocks = jnp.concatenate(
            [blocks[:, :part]]
            + [swap(blocks[:, i * part : (i + 1) * part], i << shift) for i in range(1, size)],
            axis=0,
        )
    return blocks


def scatter(blocks, plan):
    for shift, size in plan:
        part = blocks.shape[0] // size
        total = blocks[:part]
        for i in range(1, size):
            sent = blocks[i * part : (i + 1) * part].astype(BF)
            total = total + swap(sent, i << shift).astype(F32)
        blocks = total
    return blocks


def call(kernel, out_shape, args, specs=None, scratch=(), mib=24, flops=0, nbytes=0):
    return pl.pallas_call(
        kernel,
        out_shape=out_shape,
        in_specs=specs or [VMEM] * len(args),
        out_specs=jax.tree.map(lambda _: VMEM, out_shape),
        scratch_shapes=list(scratch),
        compiler_params=pltpu.CompilerParams(vmem_limit_bytes=mib << 20),
        cost_estimate=pl.CostEstimate(flops=flops, bytes_accessed=nbytes, transcendentals=0),
    )(*args)


def in_hbm(*arrays):
    return tuple(pltpu.with_memory_space_constraint(a, pltpu.HBM) for a in arrays)


def stage(parts, *refs):
    count = len(parts)
    sources = [r if p is None else r.at[p] for r, p in zip(refs[1 : 1 + count], parts)]
    copies = fetch(list(zip(sources, refs[1 + count : -1])), refs[-1])
    for copy in copies:
        copy.wait()


def staged(after, *pairs):
    arrays, parts = zip(*[p if isinstance(p, tuple) else (p, None) for p in pairs])
    shapes = [a.shape if p is None else a.shape[1:] for a, p in zip(arrays, parts)]
    return call(
        functools.partial(stage, parts),
        tuple(pltpu.VMEM(shape, a.dtype) for shape, a in zip(shapes, arrays)),
        (after,) + in_hbm(*arrays),
        specs=[HBM] * (1 + len(arrays)),
        scratch=(pltpu.SemaphoreType.DMA((len(arrays),)),),
        mib=1,
        nbytes=sum(2 * math.prod(shape) for shape in shapes),
    )


def fetch(pairs, sem):
    copies = [pltpu.make_async_copy(a, b, sem.at[i]) for i, (a, b) in enumerate(pairs)]
    for copy in copies:
        copy.start()
    return copies


def cos_sin(angle):
    turns = jnp.floor(angle * (2.0 / 3.141592653589793) + 0.5)
    rest = angle - turns * 1.5703125
    rest = rest - turns * 4.837512969970703125e-4
    rest = rest - turns * 7.54978995489188216e-8
    square = rest * rest
    sine = ((-1.9515295891e-4 * square + 8.3321608736e-3) * square - 1.6666654611e-1) * square
    sine = sine * rest + rest
    cosine = (2.443315711809948e-5 * square - 1.388731625493765e-3) * square + 4.166664568298827e-2
    cosine = cosine * square * square - 0.5 * square + 1.0
    turns = turns.astype(I32)
    odd = (turns & 1) == 1
    cosine, sine = jnp.where(odd, sine, cosine), jnp.where(odd, cosine, sine)
    cosine = jnp.where(((turns + 1) & 2) == 2, -cosine, cosine)
    sine = jnp.where((turns & 2) == 2, -sine, sine)
    return cosine, sine


def project(
    lengths_hbm, freq_hbm, ids_hbm, route_hbm, hidden_hbm, gain_hbm, weight_hbm, out_ref, turn_ref, norm_ref,
    lengths, freq, ids, routes, hidden, gain, weight, sem,
):
    chunks = sem.shape[0] - 6
    deep = weight.shape[0] // chunks
    parts = [pl.ds(i * deep, deep) for i in range(chunks)]
    copies = fetch(
        [
            (lengths_hbm, lengths),
            (freq_hbm, freq),
            (ids_hbm, ids),
            (route_hbm, routes),
            (hidden_hbm, hidden),
            (gain_hbm, gain),
        ]
        + [(weight_hbm.at[p], weight.at[p]) for p in parts],
        sem,
    )
    width = weight.shape[1]
    rows = hidden.shape[0]
    copies[0].wait()
    copies[1].wait()
    diagonal = lax.broadcasted_iota(I32, (rows, rows), 0) == lax.broadcasted_iota(
        I32, (rows, rows), 1
    )
    positions = jnp.sum(
        jnp.where(diagonal, lengths[...].astype(F32), 0.0), axis=1, keepdims=True
    )
    cosine, sine = cos_sin(positions * freq[...])
    sine = jnp.where(lax.broadcasted_iota(I32, sine.shape, 1) < HD // 2, -sine, sine)
    turn_ref[:, :HD] = cosine
    turn_ref[:, HD : 2 * HD] = sine
    core = lax.axis_index(HEAD[1]).astype(F32)
    turn_ref[:, 2 * HD :] = jnp.broadcast_to(core, (rows, HD))
    copies[2].wait()
    copies[3].wait()
    route = routes[...]
    heavy = route.astype(BF).astype(F32)
    lines = jnp.concatenate([ids[...].astype(F32), heavy, route - heavy], axis=0).astype(BF)
    shape = (lines.shape[0], HD)
    eye = lax.broadcasted_iota(I32, shape, 0) == lax.broadcasted_iota(I32, shape, 1)
    out_ref[:, width:] = lax.dot_general(
        lines, jnp.where(eye, 1.0, 0.0).astype(BF), TN, preferred_element_type=F32
    ).astype(BF)
    copies[4].wait()
    copies[5].wait()
    normed = rms_scale(hidden[...].astype(F32), gain[...]).astype(BF)
    norm_ref[...] = normed
    query = jnp.zeros((rows, width), F32)
    for i in range(chunks):
        copies[6 + i].wait()
        part = slice(i * deep, (i + 1) * deep)
        query = query + jnp.dot(normed[:, part], weight[part], preferred_element_type=F32)
    for i in range(width // HD):
        part = query[:, i * HD : (i + 1) * HD]
        turned = part * cosine + pltpu.roll(part, HD // 2, 1) * sine
        out_ref[:, i * HD : (i + 1) * HD] = turned.astype(BF)


def attend(
    query_ref, column_ref, row_ref, fill_ref, keys, values, out_ref,
    scores, probs, out_buf,
):
    pages = keys.shape[0]
    rows = query_ref.shape[0]
    lines = pages * QPK
    slots = keys.shape[1]
    hot = lax.broadcasted_iota(I32, (lines, QPK * rows), 1) == column_ref[...]
    stacked = jnp.concatenate([query_ref[:, i * HD : (i + 1) * HD] for i in range(QPK)], axis=0)
    query = jnp.dot(
        jnp.where(hot, 1.0, 0.0).astype(BF), stacked, preferred_element_type=F32
    ).astype(BF)
    some = 4
    span = some * slots
    for g in range(pages // some):
        part = slice(g * some * QPK, (g + 1) * some * QPK)
        key = keys[g * some : (g + 1) * some].reshape(span, HD)
        scores[part] = lax.dot_general(query[part], key, NT, preferred_element_type=F32)
    slot = lax.broadcasted_iota(I32, (lines, span), 1)
    first = (lax.broadcasted_iota(I32, (lines, 1), 0) // QPK) % some * slots
    live = (slot >= first) & (slot < first + fill_ref[...])
    score = jnp.where(live, scores[...] * (HD ** (-0.5)), NEG_LARGE)
    page_max = jnp.max(score, axis=1, keepdims=True)
    prob = jnp.where(live, jnp.exp(score - page_max), 0.0).astype(BF)
    probs[...] = prob
    page_sum = jnp.sum(prob.astype(F32), axis=1, keepdims=True)
    for g in range(pages // some):
        part = slice(g * some * QPK, (g + 1) * some * QPK)
        value = values[g * some : (g + 1) * some].reshape(span, HD)
        out_buf[part] = jnp.dot(probs[part], value, preferred_element_type=F32)
    held_max = jnp.max(jnp.where(hot, page_max, NEG_LARGE), axis=0, keepdims=True)
    back = jnp.sum(jnp.where(hot, held_max, 0.0), axis=1, keepdims=True)
    weight = jnp.exp(page_max - back)
    held_sum = jnp.sum(jnp.where(hot, page_sum * weight, 0.0), axis=0, keepdims=True)
    turned = lax.broadcasted_iota(I32, (QPK * rows, lines), 0) == row_ref[...]
    held_out = jnp.dot(
        jnp.where(turned, 1.0, 0.0).astype(BF),
        (out_buf[...] * weight).astype(BF),
        preferred_element_type=F32,
    )
    for i in range(QPK):
        out_ref[:, i * HD : (i + 1) * HD] = held_out[i * rows : (i + 1) * rows].astype(BF)
    rest = jnp.concatenate(
        [held_max[:, i * rows : (i + 1) * rows] for i in range(QPK)]
        + [held_sum[:, i * rows : (i + 1) * rows] for i in range(QPK)],
        axis=0,
    )
    terms = []
    for _ in range(3):
        term = rest.astype(BF).astype(F32)
        terms.append(term)
        rest = rest - term
    terms.append(jnp.zeros((HD - 6 * QPK, rows), F32))
    out_ref[:, QPK * HD :] = jnp.concatenate(terms, axis=0).T.astype(BF)


def combine(
    came_ref, query_ref, kv_ref, weight_ref, keep_ref, send_ref
):
    sources, rows = came_ref.shape[0], came_ref.shape[1]
    stats = came_ref[:, :, QPK * HD :].astype(F32).reshape(sources * rows, HD)
    step = 2 * QPK
    stats = stats[:, :step] + stats[:, step : 2 * step] + stats[:, 2 * step : 3 * step]
    stats = stats.reshape(sources, rows, step)
    part_max, part_sum = stats[:, :, :QPK], stats[:, :, QPK:]
    own_max = jnp.max(part_max, axis=0)
    key = kv_ref[:, :HD].astype(F32)
    value = kv_ref[:, HD:].astype(F32)
    new_score = jnp.concatenate(
        [
            jnp.sum(query_ref[:, i * HD : (i + 1) * HD].astype(F32) * key, axis=1, keepdims=True)
            for i in range(QPK)
        ],
        axis=1,
    ) * (HD ** (-0.5))
    top = jnp.maximum(own_max, new_score)
    new_scale = jnp.exp(new_score - top)
    scale = jnp.exp(part_max - top[None])
    denominator = jnp.sum(scale * part_sum, axis=0) + new_scale
    attention = []
    for i in range(QPK):
        total = new_scale[:, i : i + 1] * value
        for s in range(sources):
            total = total + scale[s, :, i : i + 1] * came_ref[
                s, :, i * HD : (i + 1) * HD
            ].astype(F32)
        attention.append((total / denominator[:, i : i + 1]).astype(BF))
    wide = jnp.dot(
        jnp.concatenate(attention, axis=1), weight_ref[...], preferred_element_type=F32
    )
    keep_ref[...] = wide
    send_ref[...] = wide.astype(BF)


def shared_kernel(
    residual_ref, gain_ref, gate_ref, down_ref, up_hbm, out_ref, up_ref, sem
):
    copies = fetch(((up_hbm.at[1], up_ref),), sem)
    inputs = rms_scale(residual_ref[...], gain_ref[...]).astype(BF)
    gate = lax.dot_general(inputs, gate_ref[...], NT, preferred_element_type=F32)
    copies[0].wait()
    up = lax.dot_general(inputs, up_ref[...], NT, preferred_element_type=F32)
    act = (jax.nn.silu(gate) * up).astype(BF)
    out_ref[...] = jnp.dot(act, down_ref[...], preferred_element_type=F32)


def blocks_of(step):
    head = index_of(HEAD)
    return lambda i, size: pl.ds(pl.multiple_of((head ^ (2 * i + step)) * size, HD), size)


def down_product(acts, down, shared_ref, out_ref, step):
    few = shared_ref.shape[0]
    size = out_ref.shape[2]
    place = blocks_of(step)
    for i in range(out_ref.shape[0]):
        at = place(i, size)
        out = sum(
            jnp.dot(act[...], down[e, :, at], preferred_element_type=F32)
            for e, act in enumerate(acts)
        )
        out_ref[i, :few] = (out[:few] + shared_ref[:, at]).astype(out_ref.dtype)
        out_ref[i, few:] = out[few:].astype(out_ref.dtype)


def keep_kernel(acts_ref, down_ref, shared_ref, keep_ref):
    acts = [acts_ref.at[e] for e in range(acts_ref.shape[0])]
    down_product(acts, down_ref, shared_ref, keep_ref, 0)


def experts_kernel(routes, count, *refs):
    here, there, here_other, there_other, gain_ref, routing_ref, shared_ref = refs[:7]
    expert_up = refs[7 : 7 + count]
    down_hbm, send_ref, acts_ref, down_ref, inputs, squares, sem = refs[7 + count :]
    copies = fetch([(down_hbm.at[e], down_ref.at[e]) for e in range(count)], sem)
    lines, size = here.shape
    core = lax.axis_index(HEAD[1])
    few = shared_ref.shape[0]
    squares[...] = jnp.zeros(squares.shape, F32)

    def put(rows, columns, values):
        values = values.astype(F32)
        squares[rows] += jnp.sum(values * values, axis=1, keepdims=True)
        inputs[rows, columns] = (values * gain_ref[:, columns]).astype(BF)

    for y, pair in enumerate(((here, here_other), (there, there_other))):
        for c, ref in zip((core, 1 - core), pair):
            half = pl.ds(pl.multiple_of(c * size, HD), size)
            for k in range(0, lines, 4 * few):
                row = y * lines + k
                third = pl.ds(pl.multiple_of(row + (2 + c) * few, 16), few)
                put(pl.ds(row, few), half, ref[k : k + few])
                put(third, pl.ds(0, size), ref[k + few : k + 2 * few])
                put(third, pl.ds(size, size), ref[k + 2 * few : k + 3 * few])
                put(pl.ds(row + few, few), half, ref[k + 3 * few : k + 4 * few])
    scale = lax.rsqrt(squares[:, :1] / (2 * size) + EPSILON)
    routing = routing_ref[...].astype(F32)
    ids = routing[:, :routes]
    weights = routing[:, routes : 2 * routes] + routing[:, 2 * routes : 3 * routes]
    for e in range(count):
        index = (index_of(REQ) * count + e).astype(F32)
        factor = jnp.sum(jnp.where(ids == index, weights, 0.0), axis=1, keepdims=True)
        gate = lax.dot_general(inputs[...], expert_up[e][0], NT, preferred_element_type=F32)
        up = lax.dot_general(inputs[...], expert_up[e][1], NT, preferred_element_type=F32)
        act = jax.nn.silu(gate * scale) * (up * scale) * factor
        acts_ref[e] = act.astype(BF)
    for copy in copies:
        copy.wait()
    acts = [acts_ref.at[e] for e in range(count)]
    down_product(acts, down_ref, shared_ref, send_ref, 1)


def local(
    hidden_in,
    lengths,
    page_request,
    page_fill,
    cache_keys,
    cache_values,
    attn_gain,
    query_weight,
    keyval_weight,
    out_weight,
    moe_gain,
    shared_gate_up,
    shared_down,
    expert_gate_up,
    expert_down,
    expert_ids,
    route_weights,
):
    rows, width = hidden_in.shape
    req_count = size_of(REQ)
    head_count = size_of(HEAD)
    req = index_of(REQ)
    wide = QPK * HD
    all_rows = rows * req_count
    pages = page_request.shape[0]
    top = expert_ids.shape[1]
    quarter = width // head_count
    plan = stages(req_count, 2)
    far = head_count // 2

    half = HD // 2
    frequency = np.tile(ROPE_BASE ** (-2.0 * np.arange(half) / HD), 2).astype(np.float32)[None]

    def vmem(*shape, dtype=BF):
        return pltpu.VMEM(shape, dtype)

    inputs = in_hbm(
        lengths[None],
        jnp.asarray(frequency),
        expert_ids.T,
        route_weights.T,
        hidden_in,
        attn_gain[None],
        query_weight,
    )
    packed, turn, normed = call(
        project,
        (
            jax.ShapeDtypeStruct((rows, wide + HD), BF),
            jax.ShapeDtypeStruct((rows, 3 * HD), F32),
            jax.ShapeDtypeStruct((rows, width), BF),
        ),
        inputs,
        specs=[HBM] * 7,
        scratch=tuple(pltpu.VMEM(a.shape, a.dtype) for a in inputs)
        + (pltpu.SemaphoreType.DMA((10,)),),
        flops=2 * rows * width * wide,
        nbytes=2 * width * wide,
    )
    shape = (pages, cache_keys.shape[2], HD)
    near = gather(packed, plan[1:])
    keyval = jnp.einsum("rd,dkc->rkc", normed, keyval_weight, preferred_element_type=F32)
    new_key = keyval[:, 0]
    new_key = new_key * turn[:, :HD] + jnp.roll(new_key, half, axis=1) * turn[:, HD : 2 * HD]
    new_kv = jnp.concatenate([new_key, keyval[:, 1]], axis=1).astype(BF)
    near, new_kv = joined(near, new_kv)
    keys, values = staged(near, cache_keys.reshape(shape), cache_values.reshape(shape))
    gathered = gather(near, plan[:1])

    place = position((page_request // rows) ^ req, plan) * rows + page_request % rows
    block = jnp.arange(QPK, dtype=I32)[None, :] * all_rows
    column = (block + place[:, None]).reshape(-1)
    fill = jnp.repeat(page_fill, QPK)
    partial = call(
        attend,
        jax.ShapeDtypeStruct((all_rows, wide + HD), BF),
        (gathered, column[:, None], column[None, :], fill[:, None], keys, values),
        scratch=(
            vmem(pages * QPK, 4 * shape[1], dtype=F32),
            vmem(pages * QPK, 4 * shape[1]),
            vmem(pages * QPK, HD, dtype=F32),
        ),
        flops=4 * pages * QPK * 4 * shape[1] * HD,
        nbytes=4 * pages * shape[1] * HD,
    )
    shared_up = jnp.transpose(shared_gate_up, (1, 2, 0))
    expert_up = jnp.transpose(expert_gate_up, (0, 2, 3, 1))
    experts = expert_up.shape[0]
    early = experts // 2
    out_w, *ups = staged(partial, out_weight, *[(expert_up, e) for e in range(early)])
    came = deliver(partial[None], plan[:1])
    came, out_w, *ups = joined(came, out_w, *ups)
    ups += staged(came, *[(expert_up, e) for e in range(early, experts)])
    came = deliver(came, plan[1:])
    came, *ups = joined(came, *ups)

    keep, send = call(
        combine,
        (jax.ShapeDtypeStruct((rows, width), F32), jax.ShapeDtypeStruct((rows, width), BF)),
        (came, packed, new_kv, out_w),
        flops=2 * rows * wide * width,
        nbytes=2 * wide * width,
        mib=8,
    )
    keep = keep + swap(send, 0, 1).astype(F32)
    sent = keep.astype(BF)
    (shared_down,) = staged(sent, shared_down)
    residual = keep + hidden_in.astype(F32)
    for i in range(1, far):
        residual = residual + swap(sent, 0, 2 * i).astype(F32)
    residual, shared_down = joined(residual, shared_down)

    (gate_w,) = staged(residual, (shared_up, 0))
    core = turn[:, 2 * HD : 2 * HD + 1]
    half_width = width // 2
    low = residual.astype(BF)
    sides = (low[:, :half_width], low[:, half_width:])
    here = trade(
        jnp.concatenate(sides, axis=0), jnp.where(core > 0.5, sides[1], sides[0]), plan[-1][0]
    )
    here = gather(here, plan[1:-1])
    here, late, gate_w = joined(here, residual, gate_w)
    there = swap(here, 1)
    here_other = swap(here, 0, 1)
    shared = call(
        shared_kernel,
        jax.ShapeDtypeStruct((rows, width), F32),
        (late, moe_gain[None], gate_w, shared_down) + in_hbm(shared_up),
        specs=[VMEM] * 4 + [HBM],
        scratch=(vmem(*shared_down.shape), pltpu.SemaphoreType.DMA((1,))),
        flops=6 * rows * width * shared_down.shape[0],
        nbytes=6 * width * shared_down.shape[0],
        mib=12,
    )
    there, shared = joined(there, shared)
    there_other = swap(there, 0, 1)

    small = (here, there, here_other, there_other, moe_gain[None], gathered[:, wide:], shared)
    blocks = (far, all_rows, quarter)
    send, acts, down = call(
        functools.partial(experts_kernel, top, experts),
        (
            jax.ShapeDtypeStruct(blocks, BF),
            jax.ShapeDtypeStruct((experts, all_rows, expert_down.shape[1]), BF),
            pltpu.VMEM(expert_down.shape, BF),
        ),
        small + tuple(ups) + in_hbm(expert_down),
        specs=[VMEM] * (7 + experts) + [HBM],
        scratch=(
            vmem(all_rows, width),
            vmem(all_rows, HD, dtype=F32),
            pltpu.SemaphoreType.DMA((experts,)),
        ),
        flops=5 * all_rows * width * 2 * expert_down.shape[1],
        nbytes=5 * width * 2 * expert_down.shape[1],
    )
    keep = call(
        keep_kernel,
        jax.ShapeDtypeStruct(blocks, F32),
        (acts, down, shared),
        flops=all_rows * width * 2 * expert_down.shape[1],
        nbytes=width * 2 * expert_down.shape[1],
        mib=16,
    )
    keep = keep + swap(send, 0, 1).astype(F32)
    part = all_rows // 2
    total = keep[0, :part]
    for i in range(far):
        for j in range(2):
            if i or j:
                sent = keep[i, j * part : (j + 1) * part].astype(BF)
                total = total + swap(sent, j, 2 * i).astype(F32)
    total = scatter(total, plan[1:])
    own = lax.dynamic_slice_in_dim(residual, index_of(HEAD) * quarter, quarter, 1)
    return (own + total).astype(BF)


def solution(mesh):
    in_specs = (
        P("req", None),
        P("req"),
        P("req"),
        P("req"),
        P("req", "head", None, None),
        P("req", "head", None, None),
        P(),
        P(None, "head"),
        P(None, None, "head"),
        P("head", None),
        P(),
        P(None, None, "head"),
        P("head", None),
        P("req", None, None, "head"),
        P("req", "head", None),
        P("req", None),
        P("req", None),
    )
    out_specs = P("req", "head")
    shape = (mesh.shape["req"] // 2, 2, mesh.shape["head"] // 2, 2)
    split = Mesh(mesh.devices.reshape(shape), REQ + HEAD)
    names = {"req": REQ, "head": HEAD}
    in_specs, out_specs = jax.tree.map(
        lambda spec: P(*(names.get(n) for n in spec)),
        (in_specs, out_specs),
        is_leaf=lambda spec: isinstance(spec, P),
    )
    return jax.shard_map(local, mesh=split, in_specs=in_specs, out_specs=out_specs, check_vma=False)
```

```python
import functools
import math

import jax
import jax.numpy as jnp
import numpy as np
from jax import lax
from jax.experimental import pallas as pl
from jax.experimental.pallas import tpu as pltpu
from jax.sharding import Mesh
from jax.sharding import PartitionSpec as P

QPK = 4
HD = 128

EPSILON = 1e-06
ROPE_BASE = 600000.0
NEG_LARGE = -1e30
BF = jnp.bfloat16
F32 = jnp.float32
I32 = jnp.int32
VMEM = pl.BlockSpec(memory_space=pltpu.VMEM)
HBM = pl.BlockSpec(memory_space=pltpu.HBM)
REQ = ("ru", "rl")
HEAD = ("hu", "hl")
NT = (((1,), (1,)), ((), ()))
TN = (((0,), (0,)), ((), ()))


def rms_scale(values, gain_vector):
    return (
        values
        * lax.rsqrt(jnp.mean(values * values, axis=-1, keepdims=True) + EPSILON)
        * gain_vector
    )


def index_of(axes):
    return lax.axis_index(axes[0]) * lax.axis_size(axes[1]) + lax.axis_index(axes[1])


def size_of(axes):
    return lax.axis_size(axes[0]) * lax.axis_size(axes[1])


def swap(value, req_step, head_step=0):
    heads = size_of(HEAD)
    count = size_of(REQ) * heads
    step = req_step * heads + head_step
    return lax.ppermute(value, REQ + HEAD, [(i, i ^ step) for i in range(count)])


def stages(count, first):
    found, shift = [], 0
    while count > 1:
        size = min(count, 4 if shift else first)
        found.append((shift, size))
        shift += size.bit_length() - 1
        count //= size
    return found


def trade(whole, half, shift):
    heads = size_of(HEAD)
    count = size_of(REQ) * heads
    steps = [(2 << shift) * heads, (3 << shift) * heads]
    came = lax.ppermute(whole, REQ + HEAD, [(i, i ^ steps[i % 2]) for i in range(count)])
    return jnp.concatenate([half, came, swap(half, 1 << shift)], axis=0)


def position(index, plan):
    place, scale = 0, 1
    for shift, size in reversed(plan):
        place = place + ((index >> shift) & (size - 1)) * scale
        scale *= size
    return place


def gather(block, plan):
    for shift, size in reversed(plan):
        block = jnp.concatenate(
            [block] + [swap(block, i << shift) for i in range(1, size)], axis=0
        )
    return block


def joined(*arrays):
    return lax.optimization_barrier(arrays)


def deliver(blocks, plan):
    for shift, size in plan:
        part = blocks.shape[1] // size
        blocks = jnp.concatenate(
            [blocks[:, :part]]
            + [swap(blocks[:, i * part : (i + 1) * part], i << shift) for i in range(1, size)],
            axis=0,
        )
    return blocks


def scatter(blocks, plan):
    for shift, size in plan:
        part = blocks.shape[0] // size
        total = blocks[:part]
        for i in reversed(range(1, size)):
            sent = blocks[i * part : (i + 1) * part].astype(BF)
            total = total + swap(sent, i << shift).astype(F32)
        blocks = total
    return blocks


def call(kernel, out_shape, args, specs=None, scratch=(), mib=24, flops=0, nbytes=0):
    return pl.pallas_call(
        kernel,
        out_shape=out_shape,
        in_specs=specs or [VMEM] * len(args),
        out_specs=jax.tree.map(lambda _: VMEM, out_shape),
        scratch_shapes=list(scratch),
        compiler_params=pltpu.CompilerParams(vmem_limit_bytes=mib << 20),
        cost_estimate=pl.CostEstimate(flops=flops, bytes_accessed=nbytes, transcendentals=0),
    )(*args)


def in_hbm(*arrays):
    return tuple(pltpu.with_memory_space_constraint(a, pltpu.HBM) for a in arrays)


def stage(parts, *refs):
    count = len(parts)
    sources = [r if p is None else r.at[p] for r, p in zip(refs[1 : 1 + count], parts)]
    copies = fetch(list(zip(sources, refs[1 + count : -1])), refs[-1])
    for copy in copies:
        copy.wait()


def staged(after, *pairs):
    arrays, parts = zip(*[p if isinstance(p, tuple) else (p, None) for p in pairs])
    shapes = [a.shape if p is None else a.shape[1:] for a, p in zip(arrays, parts)]
    return call(
        functools.partial(stage, parts),
        tuple(pltpu.VMEM(shape, a.dtype) for shape, a in zip(shapes, arrays)),
        (after,) + in_hbm(*arrays),
        specs=[HBM] * (1 + len(arrays)),
        scratch=(pltpu.SemaphoreType.DMA((len(arrays),)),),
        mib=1,
        nbytes=sum(2 * math.prod(shape) for shape in shapes),
    )


def fetch(pairs, sem):
    copies = [pltpu.make_async_copy(a, b, sem.at[i]) for i, (a, b) in enumerate(pairs)]
    for copy in copies:
        copy.start()
    return copies


def cos_sin(angle):
    turns = jnp.floor(angle * (2.0 / 3.141592653589793) + 0.5)
    rest = angle - turns * 1.5703125
    rest = rest - turns * 4.837512969970703125e-4
    rest = rest - turns * 7.54978995489188216e-8
    square = rest * rest
    sine = ((-1.9515295891e-4 * square + 8.3321608736e-3) * square - 1.6666654611e-1) * square
    sine = sine * rest + rest
    cosine = (2.443315711809948e-5 * square - 1.388731625493765e-3) * square + 4.166664568298827e-2
    cosine = cosine * square * square - 0.5 * square + 1.0
    turns = turns.astype(I32)
    odd = (turns & 1) == 1
    cosine, sine = jnp.where(odd, sine, cosine), jnp.where(odd, cosine, sine)
    cosine = jnp.where(((turns + 1) & 2) == 2, -cosine, cosine)
    sine = jnp.where((turns & 2) == 2, -sine, sine)
    return cosine, sine


def project(
    lengths_hbm, freq_hbm, ids_hbm, route_hbm, hidden_hbm, gain_hbm, weight_hbm, out_ref, turn_ref, norm_ref,
    lengths, freq, ids, routes, hidden, gain, weight, sem,
):
    chunks = sem.shape[0] - 6
    deep = weight.shape[0] // chunks
    parts = [pl.ds(i * deep, deep) for i in range(chunks)]
    copies = fetch(
        [
            (lengths_hbm, lengths),
            (freq_hbm, freq),
            (ids_hbm, ids),
            (route_hbm, routes),
            (hidden_hbm, hidden),
            (gain_hbm, gain),
        ]
        + [(weight_hbm.at[p], weight.at[p]) for p in parts],
        sem,
    )
    width = weight.shape[1]
    rows = hidden.shape[0]
    copies[0].wait()
    copies[1].wait()
    diagonal = lax.broadcasted_iota(I32, (rows, rows), 0) == lax.broadcasted_iota(
        I32, (rows, rows), 1
    )
    positions = jnp.sum(
        jnp.where(diagonal, lengths[...].astype(F32), 0.0), axis=1, keepdims=True
    )
    cosine, sine = cos_sin(positions * freq[...])
    sine = jnp.where(lax.broadcasted_iota(I32, sine.shape, 1) < HD // 2, -sine, sine)
    turn_ref[:, :HD] = cosine
    turn_ref[:, HD : 2 * HD] = sine
    core = lax.axis_index(HEAD[1]).astype(F32)
    turn_ref[:, 2 * HD :] = jnp.broadcast_to(core, (rows, HD))
    copies[2].wait()
    copies[3].wait()
    route = routes[...]
    heavy = route.astype(BF).astype(F32)
    lines = jnp.concatenate([ids[...].astype(F32), heavy, route - heavy], axis=0).astype(BF)
    shape = (lines.shape[0], HD)
    eye = lax.broadcasted_iota(I32, shape, 0) == lax.broadcasted_iota(I32, shape, 1)
    out_ref[:, width:] = lax.dot_general(
        lines, jnp.where(eye, 1.0, 0.0).astype(BF), TN, preferred_element_type=F32
    ).astype(BF)
    copies[4].wait()
    copies[5].wait()
    normed = rms_scale(hidden[...].astype(F32), gain[...]).astype(BF)
    norm_ref[...] = normed
    query = jnp.zeros((rows, width), F32)
    for i in range(chunks):
        copies[6 + i].wait()
        part = slice(i * deep, (i + 1) * deep)
        query = query + jnp.dot(normed[:, part], weight[part], preferred_element_type=F32)
    for i in range(width // HD):
        part = query[:, i * HD : (i + 1) * HD]
        turned = part * cosine + pltpu.roll(part, HD // 2, 1) * sine
        out_ref[:, i * HD : (i + 1) * HD] = turned.astype(BF)


def attend(
    query_ref, column_ref, row_ref, fill_ref, keys, values, out_ref,
    scores, probs, out_buf,
):
    pages = keys.shape[0]
    rows = query_ref.shape[0]
    lines = pages * QPK
    slots = keys.shape[1]
    hot = lax.broadcasted_iota(I32, (lines, QPK * rows), 1) == column_ref[...]
    stacked = jnp.concatenate([query_ref[:, i * HD : (i + 1) * HD] for i in range(QPK)], axis=0)
    query = jnp.dot(
        jnp.where(hot, 1.0, 0.0).astype(BF), stacked, preferred_element_type=F32
    ).astype(BF)
    some = 4
    span = some * slots
    for g in range(pages // some):
        part = slice(g * some * QPK, (g + 1) * some * QPK)
        key = keys[g * some : (g + 1) * some].reshape(span, HD)
        scores[part] = lax.dot_general(query[part], key, NT, preferred_element_type=F32)
    slot = lax.broadcasted_iota(I32, (lines, span), 1)
    first = (lax.broadcasted_iota(I32, (lines, 1), 0) // QPK) % some * slots
    live = (slot >= first) & (slot < first + fill_ref[...])
    score = jnp.where(live, scores[...] * (HD ** (-0.5)), NEG_LARGE)
    page_max = jnp.max(score, axis=1, keepdims=True)
    prob = jnp.where(live, jnp.exp(score - page_max), 0.0).astype(BF)
    probs[...] = prob
    page_sum = jnp.sum(prob.astype(F32), axis=1, keepdims=True)
    for g in range(pages // some):
        part = slice(g * some * QPK, (g + 1) * some * QPK)
        value = values[g * some : (g + 1) * some].reshape(span, HD)
        out_buf[part] = jnp.dot(probs[part], value, preferred_element_type=F32)
    held_max = jnp.max(jnp.where(hot, page_max, NEG_LARGE), axis=0, keepdims=True)
    back = jnp.sum(jnp.where(hot, held_max, 0.0), axis=1, keepdims=True)
    weight = jnp.exp(page_max - back)
    held_sum = jnp.sum(jnp.where(hot, page_sum * weight, 0.0), axis=0, keepdims=True)
    turned = lax.broadcasted_iota(I32, (QPK * rows, lines), 0) == row_ref[...]
    held_out = jnp.dot(
        jnp.where(turned, 1.0, 0.0).astype(BF),
        (out_buf[...] * weight).astype(BF),
        preferred_element_type=F32,
    )
    for i in range(QPK):
        out_ref[:, i * HD : (i + 1) * HD] = held_out[i * rows : (i + 1) * rows].astype(BF)
    rest = jnp.concatenate(
        [held_max[:, i * rows : (i + 1) * rows] for i in range(QPK)]
        + [held_sum[:, i * rows : (i + 1) * rows] for i in range(QPK)],
        axis=0,
    )
    terms = []
    for _ in range(3):
        term = rest.astype(BF).astype(F32)
        terms.append(term)
        rest = rest - term
    terms.append(jnp.zeros((HD - 6 * QPK, rows), F32))
    out_ref[:, QPK * HD :] = jnp.concatenate(terms, axis=0).T.astype(BF)


def combine(
    came_ref, query_ref, kv_ref, weight_ref, keep_ref, send_ref
):
    sources, rows = came_ref.shape[0], came_ref.shape[1]
    stats = came_ref[:, :, QPK * HD :].astype(F32).reshape(sources * rows, HD)
    step = 2 * QPK
    stats = stats[:, :step] + stats[:, step : 2 * step] + stats[:, 2 * step : 3 * step]
    stats = stats.reshape(sources, rows, step)
    part_max, part_sum = stats[:, :, :QPK], stats[:, :, QPK:]
    own_max = jnp.max(part_max, axis=0)
    key = kv_ref[:, :HD].astype(F32)
    value = kv_ref[:, HD:].astype(F32)
    new_score = jnp.concatenate(
        [
            jnp.sum(query_ref[:, i * HD : (i + 1) * HD].astype(F32) * key, axis=1, keepdims=True)
            for i in range(QPK)
        ],
        axis=1,
    ) * (HD ** (-0.5))
    top = jnp.maximum(own_max, new_score)
    new_scale = jnp.exp(new_score - top)
    scale = jnp.exp(part_max - top[None])
    denominator = jnp.sum(scale * part_sum, axis=0) + new_scale
    attention = []
    for i in range(QPK):
        total = new_scale[:, i : i + 1] * value
        for s in range(sources):
            total = total + scale[s, :, i : i + 1] * came_ref[
                s, :, i * HD : (i + 1) * HD
            ].astype(F32)
        attention.append((total / denominator[:, i : i + 1]).astype(BF))
    wide = jnp.dot(
        jnp.concatenate(attention, axis=1), weight_ref[...], preferred_element_type=F32
    )
    keep_ref[...] = wide
    send_ref[...] = wide.astype(BF)


def shared_kernel(
    residual_ref, gain_ref, gate_ref, down_ref, up_hbm, out_ref, up_ref, sem
):
    copies = fetch(((up_hbm.at[1], up_ref),), sem)
    inputs = rms_scale(residual_ref[...], gain_ref[...]).astype(BF)
    gate = lax.dot_general(inputs, gate_ref[...], NT, preferred_element_type=F32)
    copies[0].wait()
    up = lax.dot_general(inputs, up_ref[...], NT, preferred_element_type=F32)
    act = (jax.nn.silu(gate) * up).astype(BF)
    out_ref[...] = jnp.dot(act, down_ref[...], preferred_element_type=F32)


def blocks_of(step):
    head = index_of(HEAD)
    return lambda i, size: pl.ds(pl.multiple_of((head ^ (2 * i + step)) * size, HD), size)


def down_product(acts, down, shared_ref, out_ref, step):
    few = shared_ref.shape[0]
    size = out_ref.shape[2]
    place = blocks_of(step)
    for i in range(out_ref.shape[0]):
        at = place(i, size)
        out = sum(
            jnp.dot(act[...], down[e, :, at], preferred_element_type=F32)
            for e, act in enumerate(acts)
        )
        out_ref[i, :few] = (out[:few] + shared_ref[:, at]).astype(out_ref.dtype)
        out_ref[i, few:] = out[few:].astype(out_ref.dtype)


def keep_kernel(acts_ref, down_ref, shared_ref, keep_ref):
    acts = [acts_ref.at[e] for e in range(acts_ref.shape[0])]
    down_product(acts, down_ref, shared_ref, keep_ref, 0)


def experts_kernel(routes, count, *refs):
    here, there, here_other, there_other, gain_ref, routing_ref, shared_ref = refs[:7]
    expert_up = refs[7 : 7 + count]
    down_hbm, send_ref, acts_ref, down_ref, inputs, squares, sem = refs[7 + count :]
    copies = fetch([(down_hbm.at[e], down_ref.at[e]) for e in range(count)], sem)
    lines, size = here.shape
    core = lax.axis_index(HEAD[1])
    few = shared_ref.shape[0]
    squares[...] = jnp.zeros(squares.shape, F32)

    def put(rows, columns, values):
        values = values.astype(F32)
        squares[rows] += jnp.sum(values * values, axis=1, keepdims=True)
        inputs[rows, columns] = (values * gain_ref[:, columns]).astype(BF)

    for y, pair in enumerate(((here, here_other), (there, there_other))):
        for c, ref in zip((core, 1 - core), pair):
            half = pl.ds(pl.multiple_of(c * size, HD), size)
            for k in range(0, lines, 4 * few):
                row = y * lines + k
                third = pl.ds(pl.multiple_of(row + (2 + c) * few, 16), few)
                put(pl.ds(row, few), half, ref[k : k + few])
                put(third, pl.ds(0, size), ref[k + few : k + 2 * few])
                put(third, pl.ds(size, size), ref[k + 2 * few : k + 3 * few])
                put(pl.ds(row + few, few), half, ref[k + 3 * few : k + 4 * few])
    scale = lax.rsqrt(squares[:, :1] / (2 * size) + EPSILON)
    routing = routing_ref[...].astype(F32)
    ids = routing[:, :routes]
    weights = routing[:, routes : 2 * routes] + routing[:, 2 * routes : 3 * routes]
    for e in range(count):
        index = (index_of(REQ) * count + e).astype(F32)
        factor = jnp.sum(jnp.where(ids == index, weights, 0.0), axis=1, keepdims=True)
        gate = lax.dot_general(inputs[...], expert_up[e][0], NT, preferred_element_type=F32)
        up = lax.dot_general(inputs[...], expert_up[e][1], NT, preferred_element_type=F32)
        act = jax.nn.silu(gate * scale) * (up * scale) * factor
        acts_ref[e] = act.astype(BF)
    for copy in copies:
        copy.wait()
    acts = [acts_ref.at[e] for e in range(count)]
    down_product(acts, down_ref, shared_ref, send_ref, 1)


def local(
    hidden_in,
    lengths,
    page_request,
    page_fill,
    cache_keys,
    cache_values,
    attn_gain,
    query_weight,
    keyval_weight,
    out_weight,
    moe_gain,
    shared_gate_up,
    shared_down,
    expert_gate_up,
    expert_down,
    expert_ids,
    route_weights,
):
    rows, width = hidden_in.shape
    req_count = size_of(REQ)
    head_count = size_of(HEAD)
    req = index_of(REQ)
    wide = QPK * HD
    all_rows = rows * req_count
    pages = page_request.shape[0]
    top = expert_ids.shape[1]
    quarter = width // head_count
    plan = stages(req_count, 2)
    far = head_count // 2

    half = HD // 2
    frequency = np.tile(ROPE_BASE ** (-2.0 * np.arange(half) / HD), 2).astype(np.float32)[None]

    def vmem(*shape, dtype=BF):
        return pltpu.VMEM(shape, dtype)

    inputs = in_hbm(
        lengths[None],
        jnp.asarray(frequency),
        expert_ids.T,
        route_weights.T,
        hidden_in,
        attn_gain[None],
        query_weight,
    )
    packed, turn, normed = call(
        project,
        (
            jax.ShapeDtypeStruct((rows, wide + HD), BF),
            jax.ShapeDtypeStruct((rows, 3 * HD), F32),
            jax.ShapeDtypeStruct((rows, width), BF),
        ),
        inputs,
        specs=[HBM] * 7,
        scratch=tuple(pltpu.VMEM(a.shape, a.dtype) for a in inputs)
        + (pltpu.SemaphoreType.DMA((10,)),),
        flops=2 * rows * width * wide,
        nbytes=2 * width * wide,
    )
    shape = (pages, cache_keys.shape[2], HD)
    near = gather(packed, plan[1:])
    keyval = jnp.einsum("rd,dkc->rkc", normed, keyval_weight, preferred_element_type=F32)
    new_key = keyval[:, 0]
    new_key = new_key * turn[:, :HD] + jnp.roll(new_key, half, axis=1) * turn[:, HD : 2 * HD]
    new_kv = jnp.concatenate([new_key, keyval[:, 1]], axis=1).astype(BF)
    near, new_kv = joined(near, new_kv)
    keys, values = staged(near, cache_keys.reshape(shape), cache_values.reshape(shape))
    gathered = gather(near, plan[:1])

    place = position((page_request // rows) ^ req, plan) * rows + page_request % rows
    block = jnp.arange(QPK, dtype=I32)[None, :] * all_rows
    column = (block + place[:, None]).reshape(-1)
    fill = jnp.repeat(page_fill, QPK)
    partial = call(
        attend,
        jax.ShapeDtypeStruct((all_rows, wide + HD), BF),
        (gathered, column[:, None], column[None, :], fill[:, None], keys, values),
        scratch=(
            vmem(pages * QPK, 4 * shape[1], dtype=F32),
            vmem(pages * QPK, 4 * shape[1]),
            vmem(pages * QPK, HD, dtype=F32),
        ),
        flops=4 * pages * QPK * 4 * shape[1] * HD,
        nbytes=4 * pages * shape[1] * HD,
    )
    shared_up = jnp.transpose(shared_gate_up, (1, 2, 0))
    expert_up = jnp.transpose(expert_gate_up, (0, 2, 3, 1))
    experts = expert_up.shape[0]
    early = experts // 2
    out_w, *ups = staged(partial, out_weight, *[(expert_up, e) for e in range(early)])
    came = deliver(partial[None], plan[:1])
    came, out_w, *ups = joined(came, out_w, *ups)
    ups += staged(came, *[(expert_up, e) for e in range(early, experts)])
    came = deliver(came, plan[1:])
    came, *ups = joined(came, *ups)

    keep, send = call(
        combine,
        (jax.ShapeDtypeStruct((rows, width), F32), jax.ShapeDtypeStruct((rows, width), BF)),
        (came, packed, new_kv, out_w),
        flops=2 * rows * wide * width,
        nbytes=2 * wide * width,
        mib=8,
    )
    keep = keep + swap(send, 0, 1).astype(F32)
    sent = keep.astype(BF)
    (shared_down,) = staged(sent, shared_down)
    residual = keep + hidden_in.astype(F32)
    for i in range(1, far):
        residual = residual + swap(sent, 0, 2 * i).astype(F32)
    residual, shared_down = joined(residual, shared_down)

    (gate_w,) = staged(residual, (shared_up, 0))
    core = turn[:, 2 * HD : 2 * HD + 1]
    half_width = width // 2
    low = residual.astype(BF)
    sides = (low[:, :half_width], low[:, half_width:])
    here = trade(
        jnp.concatenate(sides, axis=0), jnp.where(core > 0.5, sides[1], sides[0]), plan[-1][0]
    )
    here = gather(here, plan[1:-1])
    here, late, gate_w = joined(here, residual, gate_w)
    there = swap(here, 1)
    here_other = swap(here, 0, 1)
    shared = call(
        shared_kernel,
        jax.ShapeDtypeStruct((rows, width), F32),
        (late, moe_gain[None], gate_w, shared_down) + in_hbm(shared_up),
        specs=[VMEM] * 4 + [HBM],
        scratch=(vmem(*shared_down.shape), pltpu.SemaphoreType.DMA((1,))),
        flops=6 * rows * width * shared_down.shape[0],
        nbytes=6 * width * shared_down.shape[0],
        mib=12,
    )
    there, shared = joined(there, shared)
    there_other = swap(there, 0, 1)

    small = (here, there, here_other, there_other, moe_gain[None], gathered[:, wide:], shared)
    blocks = (far, all_rows, quarter)
    send, acts, down = call(
        functools.partial(experts_kernel, top, experts),
        (
            jax.ShapeDtypeStruct(blocks, BF),
            jax.ShapeDtypeStruct((experts, all_rows, expert_down.shape[1]), BF),
            pltpu.VMEM(expert_down.shape, BF),
        ),
        small + tuple(ups) + in_hbm(expert_down),
        specs=[VMEM] * (7 + experts) + [HBM],
        scratch=(
            vmem(all_rows, width),
            vmem(all_rows, HD, dtype=F32),
            pltpu.SemaphoreType.DMA((experts,)),
        ),
        flops=5 * all_rows * width * 2 * expert_down.shape[1],
        nbytes=5 * width * 2 * expert_down.shape[1],
    )
    keep = call(
        keep_kernel,
        jax.ShapeDtypeStruct(blocks, F32),
        (acts, down, shared),
        flops=all_rows * width * 2 * expert_down.shape[1],
        nbytes=width * 2 * expert_down.shape[1],
        mib=16,
    )
    keep = keep + swap(send, 0, 1).astype(F32)
    part = all_rows // 2
    total = keep[0, :part]
    for i in range(far):
        for j in range(2):
            if i or j:
                sent = keep[i, j * part : (j + 1) * part].astype(BF)
                total = total + swap(sent, j, 2 * i).astype(F32)
    total = scatter(total, plan[1:])
    own = lax.dynamic_slice_in_dim(residual, index_of(HEAD) * quarter, quarter, 1)
    return (own + total).astype(BF)


def solution(mesh):
    in_specs = (
        P("req", None),
        P("req"),
        P("req"),
        P("req"),
        P("req", "head", None, None),
        P("req", "head", None, None),
        P(),
        P(None, "head"),
        P(None, None, "head"),
        P("head", None),
        P(),
        P(None, None, "head"),
        P("head", None),
        P("req", None, None, "head"),
        P("req", "head", None),
        P("req", None),
        P("req", None),
    )
    out_specs = P("req", "head")
    shape = (mesh.shape["req"] // 2, 2, mesh.shape["head"] // 2, 2)
    split = Mesh(mesh.devices.reshape(shape), REQ + HEAD)
    names = {"req": REQ, "head": HEAD}
    in_specs, out_specs = jax.tree.map(
        lambda spec: P(*(names.get(n) for n in spec)),
        (in_specs, out_specs),
        is_leaf=lambda spec: isinstance(spec, P),
    )
    return jax.shard_map(local, mesh=split, in_specs=in_specs, out_specs=out_specs, check_vma=False)
```
